128 devices in a mesh: loop: 8 (over x_lo, z), group: 16 (over y, x_hi, core).
Axes of the slice: x: 4 (x_hi: 2, x_lo: 2; x = x_hi * 2 + x_lo), y: 4, z: 4, core: 2. Of those that a mesh axis runs over, the one named last changes fastest.
Arguments:
- images: bfloat16 [16384, 1152], P(('loop', 'group')), may hold values from -1 to 1, as said below
- texts: bfloat16 [16384, 1152], P(('loop', 'group')), may hold values from -1 to 1, as said below
- logit_scale: float32 [1], replicated, may hold values from 8 to 14
- bias: float32 [1], replicated, may hold values from -6 to -3
Outputs:
- grad_images: float32 [16384, 1152], P(('loop', 'group'))
- grad_texts: float32 [16384, 1152], P(('loop', 'group'))
The draws below stay inside these ranges and needn't reach their ends.
Inputs may be any that keep to these rules, and one draw needn't show every extreme that they name: `images`: real-valued embeddings. `texts`: real-valued embeddings.
All inputs are finite; a program needn't handle non-finite values.
Results may differ from the reference program's by a relative error of at most 0.012.
Values may be sent and summed in bfloat16 or wider, within the bound.
A program may use at most 128 MiB of HBM per device.

```python
import math
import jax
import jax.numpy as jnp
from jax import lax

D = 1152
TOK_DEV = 128
STEPS = 4
TOKENS = 16384
N_LOOP = 8
N_GROUP = 16


def shared_parts(key):
    centre_key, owner_key, strength_key, pair_key, weight_key = jax.random.split(key, 5)
    clusters = max(TOKENS // 32, 1)
    centres = jnp.clip(jax.random.normal(centre_key, (clusters, D), jnp.float32), -3.0, 3.0)
    owners = jax.random.permutation(owner_key, TOKENS) % clusters
    strength = jax.random.uniform(strength_key, (clusters, 1), jnp.float32, 0.2, 0.6)
    pair_part = jnp.clip(jax.random.normal(pair_key, (TOKENS, D), jnp.float32), -3.0, 3.0)
    weights = jax.random.uniform(weight_key, (TOKENS, 1), jnp.float32, 0.1, 0.6)
    return jnp.take(strength * centres, owners, axis=0) + weights * pair_part


def draw_images(key, part):
    common_part = shared_parts(key)
    key = jax.random.fold_in(key, 11)
    first, second = jax.random.split(key, 2)
    noise = jnp.clip(jax.random.normal(first, (TOKENS, D), jnp.float32), -3.0, 3.0)
    base = common_part + noise
    scales = jnp.exp(jax.random.uniform(second, (TOKENS, 1), jnp.float32, math.log(1.0 / 3.0), math.log(3.0)))
    return (base * scales * (0.12 / math.sqrt(D))).astype(jnp.bfloat16)


def draw_texts(key, part):
    common_part = shared_parts(key)
    key = jax.random.fold_in(key, 23)
    first, second = jax.random.split(key, 2)
    noise = jnp.clip(jax.random.normal(first, (TOKENS, D), jnp.float32), -3.0, 3.0)
    base = common_part + noise
    scales = jnp.exp(jax.random.uniform(second, (TOKENS, 1), jnp.float32, math.log(1.0 / 3.0), math.log(3.0)))
    return (base * scales * (0.12 / math.sqrt(D))).astype(jnp.bfloat16)


def setup_inputs(seed: int = 0) -> dict:
    key_of = jax.random.split(jax.random.key(seed), 5)
    return {
        "images": draw_images(jax.random.fold_in(key_of[4], 71), 0),
        "texts": draw_texts(jax.random.fold_in(key_of[4], 71), 0),
        "logit_scale": jnp.clip(jax.random.uniform(key_of[2], (1,), jnp.float32, 8.0, 14.0), 8.0, 14.0),
        "bias": jnp.clip(jax.random.uniform(key_of[3], (1,), jnp.float32, -6.0, -3.0), -6.0, -3.0),
    }


def normalize(values):
    wide = values.astype(jnp.float32)
    norms = jnp.sqrt(lax.optimization_barrier(jnp.sum(wide * wide, axis=-1, keepdims=True)) + 1e-06)
    return (wide / norms, norms)

def unnormalize(normed, norms, upstream):
    inner = lax.optimization_barrier(jnp.sum(normed * upstream, axis=-1, keepdims=True))
    return (upstream - normed * inner) / norms

def pair_terms(rows, block, scale, shift, positive):
    logits = scale * jnp.dot(rows, block.T, preferred_element_type=jnp.float32) + shift
    signs = jnp.where(positive, 1.0, -1.0).astype(jnp.float32)
    slopes = (-signs * jax.nn.sigmoid(-signs * logits)).astype(jnp.bfloat16)
    dimage = scale * jnp.dot(slopes, block, preferred_element_type=jnp.float32)
    dtext = (scale * jnp.dot(slopes.T, rows, preferred_element_type=jnp.float32)).astype(jnp.bfloat16)
    return (dimage, dtext)

def reference(images, texts, logit_scale, bias):
    inormed, inorm = normalize(images)
    tnormed, tnorm = normalize(texts)
    ibf = inormed.astype(jnp.bfloat16)
    tbf = tnormed.astype(jnp.bfloat16)
    scale = logit_scale[0]
    shift = bias[0]
    blocks = tbf.reshape(N_LOOP, N_GROUP * TOK_DEV, D)
    row_ids = jnp.arange(TOK_DEV, dtype=jnp.int32)[:, None]
    col_ids = jnp.arange(N_GROUP * TOK_DEV, dtype=jnp.int32)[None, :]

    def visit(dtext, index):
        loop_at = index // N_GROUP
        group_at = index % N_GROUP
        rows = lax.dynamic_slice_in_dim(ibf, (index * TOK_DEV).astype(jnp.int32), TOK_DEV, 0)
        dimage = jnp.zeros((TOK_DEV, D), jnp.float32)
        for k in range(STEPS):
            target = ((loop_at - k) % N_LOOP).astype(jnp.int32)
            block = blocks[target]
            positive = (col_ids == group_at * TOK_DEV + row_ids) & (k == 0)
            dimg, dtxt = pair_terms(rows, block, scale, shift, positive)
            dimage = dimage + dimg
            start = (target * (N_GROUP * TOK_DEV)).astype(jnp.int32)
            current = lax.dynamic_slice_in_dim(dtext, start, N_GROUP * TOK_DEV, 0)
            dtext = lax.dynamic_update_slice_in_dim(dtext, current + dtxt.astype(jnp.float32), start, 0)
        return (dtext, dimage)
    dtext, dimages = lax.scan(visit, jnp.zeros((TOKENS, D), jnp.float32), jnp.arange(N_LOOP * N_GROUP, dtype=jnp.int32))
    dimage = dimages.reshape(TOKENS, D)
    return (unnormalize(inormed, inorm, dimage), unnormalize(tnormed, tnorm, dtext))
```

```python
import functools

import jax
import jax.numpy as jnp
from jax import lax
from jax.experimental import pallas as pl
from jax.experimental.pallas import tpu as pltpu
from jax.sharding import PartitionSpec as P

MESH = pl.DeviceIdType.MESH
ROWS = 128
HALF = 64
WIDTH = 1152
BF = jnp.bfloat16
F32 = jnp.float32


def slot_at(k, h, j):
    return k * 4 + h * 2 + j


def kernel(
    scal, images, texts, grad_images, grad_texts,
    inormed, tnormed, inorm, tnorm,
    im, tb, di, pb,
    xr, zr, o0, o1, dr, dyr,
    sx, sz, sd, sy,
    send, im_r, tb_r, xr_r, zr_r, o0_r, o1_r, dr_r, dy_r,
):
    loop = lax.axis_index("loop")
    group = lax.axis_index("group")
    x = (group // 2) % 2 * 2 + loop // 4
    z = loop % 4
    y = group // 4
    core = group % 2

    def at(dx=0, dy=0, dz=0, dc=0):
        xx = (x + dx + 8) % 4
        yy = (y + dy + 4) % 4
        zz = (z + dz + 4) % 4
        return (xx % 2 * 4 + zz, yy * 4 + xx // 2 * 2 + (core + dc) % 2)

    barrier = pltpu.get_barrier_semaphore()
    partners = [at(dc=1)]
    for d in (1, 2, 3):
        partners += [at(dx=d), at(dy=d), at(dz=d)]
    for partner in partners:
        pl.semaphore_signal(barrier, inc=1, device_id=partner, device_id_type=MESH)

    def normalize(src, normed, norm):
        wide = src[...].astype(F32)
        n = jnp.sqrt(jnp.sum(wide * wide, axis=-1, keepdims=True) + 1e-06)
        out = wide / n
        normed[...] = out
        norm[...] = n
        return out.astype(BF)

    def part(ref, slot, count=1):
        return ref.at[pl.ds(pl.multiple_of(slot * HALF, HALF), HALF * count)]

    own_text = normalize(texts, tnormed, tnorm)
    tb[0:HALF] = own_text[0:HALF]
    tb[2 * HALF:3 * HALF] = own_text[HALF:]
    im[0, core] = normalize(images, inormed, inorm)

    pl.semaphore_wait(barrier, len(partners))

    pending = []

    def put(src, dst, recv, device, cond=None):
        sem = send.at[len(pending)]

        def make():
            return pltpu.make_async_remote_copy(
                src_ref=src(), dst_ref=dst(), send_sem=sem, recv_sem=recv(),
                device_id=device, device_id_type=MESH,
            )

        pending.append((make, cond))
        if cond is None:
            make().start()
        else:
            @pl.when(cond)
            def _():
                make().start()

    def got(dst, recv, cond=None):
        def wait():
            pltpu.make_async_remote_copy(
                src_ref=dst(), dst_ref=dst(), send_sem=send.at[0], recv_sem=recv(),
                device_id=at(dc=1), device_id_type=MESH,
            ).wait_recv()

        if cond is None:
            wait()
        else:
            @pl.when(cond)
            def _():
                wait()

    def put_slot(src, dst, device, cond=None):
        put(lambda: part(tb, src), lambda: part(tb, dst), lambda: tb_r.at[dst], device, cond)

    def got_slot(slot, cond=None):
        got(lambda: part(tb, slot), lambda: tb_r.at[slot], cond)

    wraps = [(z + k >= 4).astype(jnp.int32) for k in range(4)]
    wrapped = [(z < k).astype(jnp.int32) for k in range(4)]

    put_slot(0, slot_at(0, 0, 1), at(dx=2))
    for d in (1, 3):
        put_slot(0, 16 + d // 2, at(dx=d), z > 0)
    for k in (1, 3, 2):
        s = wraps[k]
        there = s * (17 + k) + (1 - s) * slot_at(k, 1, 0)
        put_slot(2, there, at(dz=k))
    for d in (1, 3, 2):
        put(lambda: im.at[0, core], lambda d=d: im.at[d, core], lambda d=d: im_r.at[d, core], at(dy=d))
    put(lambda: im.at[0, core], lambda: im.at[0, core], lambda: im_r.at[0, core], at(dc=1))
    for k in (1, 3, 2):
        put_slot(0, slot_at(k, 0, 0), at(dz=k), wraps[k] == 0)
    put_slot(2, slot_at(0, 1, 1), at(dx=2))

    got_slot(slot_at(0, 0, 1))
    for k in (1, 3, 2):
        put_slot(slot_at(0, 0, 1), slot_at(k, 0, 1), at(dz=k), wraps[k] == 0)

    def forward_x(k):
        s = wrapped[k]
        here = s * (17 + k) + (1 - s) * slot_at(k, 1, 0)
        got_slot(here)
        put_slot(here, slot_at(k, 1, 1), at(dx=s + 2))
        put_slot(here, slot_at(k, 1, 0), at(dx=1), s == 1)

    forward_x(1)
    for d in (1, 3):
        got_slot(16 + d // 2, z > 0)
        for k in (3, 2, 1):
            put_slot(16 + d // 2, slot_at(k, 0, d // 2), at(dz=k), wraps[k] == 1)
    forward_x(3)
    forward_x(2)

    def relay_image(d):
        got(lambda: im.at[d, core], lambda: im_r.at[d, core])
        put(lambda: im.at[d, core], lambda: im.at[d, core], lambda: im_r.at[d, core], at(dc=1))

    for d in (1, 3, 2):
        relay_image(d)
    for d in (0, 1, 3, 2):
        got(lambda d=d: im.at[d, 1 - core], lambda d=d: im_r.at[d, 1 - core])

    scale = scal[0]
    shift = scal[1]

    def chunk(k, first):
        rows = pl.ds(k * 4 * HALF, 4 * HALF)
        t = tb[rows]
        i = im[...].reshape(8 * ROWS, WIDTH)
        logits = scale * lax.dot_general(t, i, (((1,), (1,)), ((), ())), preferred_element_type=F32) + shift
        if k == 0:
            r = lax.broadcasted_iota(jnp.int32, logits.shape, 0)
            c = lax.broadcasted_iota(jnp.int32, logits.shape, 1)
            own = r // (2 * HALF) * HALF + r % HALF + core * ROWS
            positive = (c == own) & (r // HALF % 2 == 0)
            signs = jnp.where(positive, 1.0, -1.0).astype(F32)
            slopes = -signs / (1.0 + jnp.exp(signs * logits))
        else:
            slopes = 1.0 / (1.0 + jnp.exp(-logits))
        slopes = slopes.astype(BF)
        pb[rows] = (scale * jnp.dot(slopes, i, preferred_element_type=F32)).astype(BF)
        term = lax.dot_general(slopes, t, (((0,), (0,)), ((), ())), preferred_element_type=F32)
        if first:
            di[...] = term
        else:
            di[...] += term

    got_slot(slot_at(0, 1, 1))
    chunk(0, True)
    put(lambda: part(pb, slot_at(0, 1, 1)), lambda: o1.at[0], lambda: o1_r.at[0], at(dx=2))

    for k in (1, 3, 2):
        s = wrapped[k]
        got_slot(slot_at(k, 0, 0))
        got_slot(slot_at(k, 0, 1))
        got_slot(slot_at(k, 1, 0), s == 1)
        got_slot(slot_at(k, 1, 1))
        chunk(k, False)
        put(lambda k=k: part(pb, slot_at(k, 0, 0), 2), lambda k=k: xr.at[k - 1], lambda k=k: xr_r.at[k - 1], at(dz=-k))
        put(lambda k=k: part(pb, slot_at(k, 1, 1)), lambda k=k: zr.at[k - 1, 1], lambda k=k: zr_r.at[k - 1, 1], at(dx=-s - 2))
        put(lambda k=k: part(pb, slot_at(k, 1, 0)), lambda k=k: zr.at[k - 1, 0], lambda k=k: zr_r.at[k - 1, 0], at(dx=-1), s == 1)

    for d in (1, 3, 2, 0):
        rows = pl.ds(pl.multiple_of(d * 2 * ROWS + (1 - core) * ROWS, ROWS), ROWS)
        sd[d] = (scale * di[rows]).astype(BF)
        put(lambda d=d: sd.at[d], lambda d=d: dr.at[d], lambda d=d: dr_r.at[d], at(dc=1))

    def mine(d):
        rows = pl.ds(pl.multiple_of(d * 2 * ROWS + core * ROWS, ROWS), ROWS)
        got(lambda: dr.at[d], lambda: dr_r.at[d])
        return scale * di[rows] + dr[d].astype(F32)

    for d in (1, 3, 2):
        sy[d - 1] = mine(d).astype(BF)
        put(lambda d=d: sy.at[d - 1], lambda d=d: dyr.at[d - 1], lambda d=d: dy_r.at[d - 1], at(dy=-d))

    def value(slot):
        return part(pb, slot)[...].astype(F32)

    for k in (1, 3, 2):
        s = wrapped[k]
        got(lambda k=k: zr.at[k - 1, 1], lambda k=k: zr_r.at[k - 1, 1])
        got(lambda k=k: zr.at[k - 1, 0], lambda k=k: zr_r.at[k - 1, 0], s == 1)

        @pl.when(s == 1)
        def _():
            sz[k - 1] = (zr[k - 1, 1].astype(F32) + zr[k - 1, 0].astype(F32)).astype(BF)

        @pl.when(s == 0)
        def _():
            sz[k - 1] = (zr[k - 1, 1].astype(F32) + value(slot_at(k, 1, 0))).astype(BF)

        put(lambda k=k: sz.at[k - 1], lambda k=k: o1.at[k], lambda k=k: o1_r.at[k], at(dz=-k))

    for k in (1, 3, 2):
        got(lambda k=k: xr.at[k - 1], lambda k=k: xr_r.at[k - 1])

    def column(j, wrap):
        total = None
        for k in (1, 2, 3):
            term = xr[k - 1, pl.ds(j * HALF, HALF)].astype(F32)
            term = jnp.where(wraps[k] == wrap, term, 0.0)
            total = term if total is None else total + term
        return total

    sx[1] = (column(1, 0) + value(slot_at(0, 0, 1))).astype(BF)
    put(lambda: sx.at[1], lambda: o0.at[1], lambda: o0_r.at[1], at(dx=-2))
    for d in (1, 3):
        @pl.when(z > 0)
        def _():
            sx[d - 1] = column(d // 2, 1).astype(BF)

        put(lambda d=d: sx.at[d - 1], lambda d=d: o0.at[d - 1], lambda d=d: o0_r.at[d - 1], at(dx=-d), z > 0)

    def unnormalize(normed, norm, upstream):
        inner = jnp.sum(normed * upstream, axis=-1, keepdims=True)
        return (upstream - normed * inner) / norm

    total = mine(0)
    for d in (1, 3, 2):
        got(lambda d=d: dyr.at[d - 1], lambda d=d: dy_r.at[d - 1])
        total = total + dyr[d - 1].astype(F32)
    grad_images[...] = unnormalize(inormed[...], inorm[...], total)

    lower = column(0, 0) + value(slot_at(0, 0, 0))
    got(lambda: o0.at[1], lambda: o0_r.at[1])
    lower = lower + o0[1].astype(F32)
    for d in (1, 3):
        got(lambda d=d: o0.at[d - 1], lambda d=d: o0_r.at[d - 1], z > 0)
        lower = lower + jnp.where(z > 0, o0[d - 1].astype(F32), 0.0)
    upper = value(slot_at(0, 1, 0))
    for k in (0, 1, 3, 2):
        got(lambda k=k: o1.at[k], lambda k=k: o1_r.at[k])
        upper = upper + o1[k].astype(F32)
    grad_texts[0:HALF] = unnormalize(tnormed[0:HALF], tnorm[0:HALF], lower)
    grad_texts[HALF:] = unnormalize(tnormed[HALF:], tnorm[HALF:], upper)

    for make, cond in pending:
        if cond is None:
            make().wait_send()
        else:
            @pl.when(cond)
            def _():
                make().wait_send()


def local(images, texts, logit_scale, bias):
    vmem = pl.BlockSpec(memory_space=pltpu.VMEM)
    dma = pltpu.SemaphoreType.DMA
    return pl.pallas_call(
        kernel,
        out_shape=[jax.ShapeDtypeStruct((ROWS, WIDTH), F32)] * 2,
        in_specs=[pl.BlockSpec(memory_space=pltpu.SMEM), vmem, vmem],
        out_specs=[vmem, vmem],
        scratch_shapes=[
            pltpu.VMEM((ROWS, WIDTH), F32),
            pltpu.VMEM((ROWS, WIDTH), F32),
            pltpu.VMEM((ROWS, 1), F32),
            pltpu.VMEM((ROWS, 1), F32),
            pltpu.VMEM((4, 2, ROWS, WIDTH), BF),
            pltpu.VMEM((21 * HALF, WIDTH), BF),
            pltpu.VMEM((8 * ROWS, WIDTH), F32),
            pltpu.VMEM((16 * HALF, WIDTH), BF),
            pltpu.VMEM((3, 2 * HALF, WIDTH), BF),
            pltpu.VMEM((3, 2, HALF, WIDTH), BF),
            pltpu.VMEM((3, HALF, WIDTH), BF),
            pltpu.VMEM((4, HALF, WIDTH), BF),
            pltpu.VMEM((4, ROWS, WIDTH), BF),
            pltpu.VMEM((3, ROWS, WIDTH), BF),
            pltpu.VMEM((3, HALF, WIDTH), BF),
            pltpu.VMEM((3, HALF, WIDTH), BF),
            pltpu.VMEM((4, ROWS, WIDTH), BF),
            pltpu.VMEM((3, ROWS, WIDTH), BF),
            dma((64,)),
            dma((4, 2)),
            dma((21,)),
            dma((3,)),
            dma((3, 2)),
            dma((3,)),
            dma((4,)),
            dma((4,)),
            dma((3,)),
        ],
        compiler_params=pltpu.CompilerParams(
            collective_id=0, has_side_effects=True, vmem_limit_bytes=56 * 2**20
        ),
        name="pair_grads",
    )(jnp.concatenate([logit_scale, bias]), images, texts)


def solution(mesh):
    in_specs = (P(("loop", "group"), None), P(("loop", "group"), None), P(), P())
    out_specs = (P(("loop", "group"), None), P(("loop", "group"), None))
    return jax.shard_map(local, mesh=mesh, in_specs=in_specs, out_specs=out_specs, check_vma=False)
```

```python
import functools

import jax
import jax.numpy as jnp
from jax import lax
from jax.experimental import pallas as pl
from jax.experimental.pallas import tpu as pltpu
from jax.sharding import PartitionSpec as P

MESH = pl.DeviceIdType.MESH
ROWS = 128
HALF = 64
WIDTH = 1152
BF = jnp.bfloat16
F32 = jnp.float32


CHUNK_AT = {2: 0, 3: 1, 0: 2, 1: 3}
IMAGE_AT = {0: 0, 1: 1, 3: 2, 2: 3}
EARLY = 6 * ROWS


def slot_at(k, h, j):
    return CHUNK_AT[k] * 4 + h * 2 + j


def kernel(
    logit_scale, bias, images_hbm, texts_hbm, grad_images, grad_texts,
    images, texts,
    inormed, tnormed, inorm, tnorm,
    im, tb, di, pt, pb,
    xr, zr, o0, o1, dr, dyr,
    sx, sz, sd, sy,
    moved, send, im_r, tb_r, xr_r, zr_r, o0_r, o1_r, dr_r, dy_r,
):
    loop = lax.axis_index("loop")
    group = lax.axis_index("group")
    x = (group // 2) % 2 * 2 + loop // 4
    z = loop % 4
    y = group // 4
    core = group % 2

    def at(dx=0, dy=0, dz=0, dc=0):
        xx = (x + dx + 8) % 4
        yy = (y + dy + 4) % 4
        zz = (z + dz + 4) % 4
        return (xx % 2 * 4 + zz, yy * 4 + xx // 2 * 2 + (core + dc) % 2)

    barrier = pltpu.get_barrier_semaphore()
    partners = [at(dc=1)]
    for d in (1, 2, 3):
        partners += [at(dx=d), at(dy=d), at(dz=d)]
    for partner in partners:
        pl.semaphore_signal(barrier, inc=1, device_id=partner, device_id_type=MESH)

    loads = [
        pltpu.make_async_copy(texts_hbm, texts, moved.at[0]),
        pltpu.make_async_copy(images_hbm, images, moved.at[1]),
    ]
    for load in loads:
        load.start()

    def normalize(src, normed, norm):
        wide = src[...].astype(F32)
        n = jnp.sqrt(jnp.sum(wide * wide, axis=-1, keepdims=True) + 1e-06)
        out = wide / n
        normed[...] = out
        norm[...] = n
        return out.astype(BF)

    def part(ref, slot, count=1):
        return ref.at[pl.ds(pl.multiple_of(slot * HALF, HALF), HALF * count)]

    loads[0].wait()
    own_text = normalize(texts, tnormed, tnorm)
    part(tb, slot_at(0, 0, 0))[...] = own_text[0:HALF]
    part(tb, slot_at(0, 1, 0))[...] = own_text[HALF:]
    loads[1].wait()
    im[0, core] = normalize(images, inormed, inorm)

    pl.semaphore_wait(barrier, len(partners))

    pending = []

    def put(src, dst, recv, device, cond=None):
        sem = send.at[len(pending)]

        def make():
            return pltpu.make_async_remote_copy(
                src_ref=src(), dst_ref=dst(), send_sem=sem, recv_sem=recv(),
                device_id=device, device_id_type=MESH,
            )

        pending.append((make, cond))
        if cond is None:
            make().start()
        else:
            @pl.when(cond)
            def _():
                make().start()

    def got(dst, recv, cond=None):
        def wait():
            pltpu.make_async_remote_copy(
                src_ref=dst(), dst_ref=dst(), send_sem=send.at[0], recv_sem=recv(),
                device_id=at(dc=1), device_id_type=MESH,
            ).wait_recv()

        if cond is None:
            wait()
        else:
            @pl.when(cond)
            def _():
                wait()

    def put_slot(src, dst, device, cond=None):
        put(lambda: part(tb, src), lambda: part(tb, dst), lambda: tb_r.at[dst], device, cond)

    def got_slot(slot, cond=None):
        got(lambda: part(tb, slot), lambda: tb_r.at[slot], cond)

    wraps = [(z + k >= 4).astype(jnp.int32) for k in range(4)]
    wrapped = [(z < k).astype(jnp.int32) for k in range(4)]

    own_low, own_high = slot_at(0, 0, 0), slot_at(0, 1, 0)

    def along_z_high(k):
        s = wraps[k]
        put_slot(own_high, s * (17 + k) + (1 - s) * slot_at(k, 1, 0), at(dz=k))

    def along_z_low(k):
        put_slot(own_low, slot_at(k, 0, 0), at(dz=k), wraps[k] == 0)

    def relay_z_near(order):
        for d in (1, 3):
            got_slot(16 + d // 2, z > 0)
            for k in order:
                put_slot(16 + d // 2, slot_at(k, 0, d // 2), at(dz=k), wraps[k] == 1)

    def relay_z_far(order):
        got_slot(slot_at(0, 0, 1))
        for k in order:
            put_slot(slot_at(0, 0, 1), slot_at(k, 0, 1), at(dz=k), wraps[k] == 0)

    def relay_x(k):
        s = wrapped[k]
        here = s * (17 + k) + (1 - s) * slot_at(k, 1, 0)
        got_slot(here)
        put_slot(here, slot_at(k, 1, 1), at(dx=s + 2))
        put_slot(here, slot_at(k, 1, 0), at(dx=1), s == 1)

    def send_image(d):
        a = IMAGE_AT[d]
        put(lambda: im.at[0, core], lambda: im.at[a, core], lambda: im_r.at[a, core], at(dy=d))

    def relay_image(d):
        a = IMAGE_AT[d]
        if d:
            got(lambda: im.at[a, core], lambda: im_r.at[a, core])
        put(lambda: im.at[a, core], lambda: im.at[a, core], lambda: im_r.at[a, core], at(dc=1))

    def got_image(d):
        a = IMAGE_AT[d]
        got(lambda: im.at[a, 1 - core], lambda: im_r.at[a, 1 - core])

    scale = logit_scale[0]
    shift = bias[0]

    def early(k, first):
        base = CHUNK_AT[k] * 4 * HALF
        rows = pl.ds(base, 4 * HALF)
        t = tb[rows]
        i = im[0:3].reshape(EARLY, WIDTH)
        logits = scale * lax.dot_general(t, i, (((1,), (1,)), ((), ())), preferred_element_type=F32) + shift
        if k == 0:
            r = lax.broadcasted_iota(jnp.int32, logits.shape, 0)
            c = lax.broadcasted_iota(jnp.int32, logits.shape, 1)
            own = r // (2 * HALF) * HALF + r % HALF + core * ROWS
            positive = (c == own) & (r // HALF % 2 == 0)
            signs = jnp.where(positive, 1.0, -1.0).astype(F32)
            slopes = -signs / (1.0 + jnp.exp(signs * logits))
        else:
            slopes = 1.0 / (1.0 + jnp.exp(-logits))
        slopes = slopes.astype(BF)
        pt[rows] = jnp.dot(slopes, i, preferred_element_type=F32)
        term = lax.dot_general(slopes, t, (((0,), (0,)), ((), ())), preferred_element_type=F32)
        if first:
            di[0:EARLY] = term
        else:
            di[0:EARLY] += term

    def late(ks, first):
        rows = pl.ds(CHUNK_AT[ks[0]] * 4 * HALF, 4 * HALF * len(ks))
        t = tb[rows]
        i = im[3].reshape(2 * ROWS, WIDTH)
        logits = scale * lax.dot_general(i, t, (((1,), (1,)), ((), ())), preferred_element_type=F32) + shift
        slopes = (1.0 / (1.0 + jnp.exp(-logits))).astype(BF)
        term = lax.dot_general(slopes, i, (((0,), (0,)), ((), ())), preferred_element_type=F32)
        pb[rows] = (scale * (pt[rows] + term)).astype(BF)
        term = jnp.dot(slopes, t, preferred_element_type=F32)
        if first:
            di[EARLY:] = term
        else:
            di[EARLY:] += term

    def value(slot):
        return part(pb, slot)[...].astype(F32)

    def got_chunk(k):
        if k == 0:
            got_slot(slot_at(0, 1, 1))
            return
        got_slot(slot_at(k, 0, 0))
        got_slot(slot_at(k, 0, 1))
        got_slot(slot_at(k, 1, 0), wrapped[k] == 1)
        got_slot(slot_at(k, 1, 1))

    def send_chunk(k):
        if k == 0:
            put(lambda: part(pb, slot_at(0, 1, 1)), lambda: o1.at[0], lambda: o1_r.at[0], at(dx=2))
            return
        s = wrapped[k]
        put(lambda: part(pb, slot_at(k, 1, 1)), lambda: zr.at[k - 1, 1], lambda: zr_r.at[k - 1, 1], at(dx=-s - 2))
        put(lambda: part(pb, slot_at(k, 1, 0)), lambda: zr.at[k - 1, 0], lambda: zr_r.at[k - 1, 0], at(dx=-1), s == 1)
        put(lambda: part(pb, slot_at(k, 0, 0), 2), lambda: xr.at[k - 1], lambda: xr_r.at[k - 1], at(dz=-k))

    def collect_z(k):
        s = wrapped[k]
        got(lambda: zr.at[k - 1, 1], lambda: zr_r.at[k - 1, 1])
        got(lambda: zr.at[k - 1, 0], lambda: zr_r.at[k - 1, 0], s == 1)

        @pl.when(s == 1)
        def _():
            sz[k - 1] = (zr[k - 1, 1].astype(F32) + zr[k - 1, 0].astype(F32)).astype(BF)

        @pl.when(s == 0)
        def _():
            sz[k - 1] = (zr[k - 1, 1].astype(F32) + value(slot_at(k, 1, 0))).astype(BF)

        put(lambda: sz.at[k - 1], lambda: o1.at[k], lambda: o1_r.at[k], at(dz=-k))

    def di_rows(d, half):
        return pl.ds(pl.multiple_of(IMAGE_AT[d] * 2 * ROWS + half * ROWS, ROWS), ROWS)

    def swap_images():
        for d in (2, 1, 3, 0):
            sd[d] = (scale * di[di_rows(d, 1 - core)]).astype(BF)
            put(lambda d=d: sd.at[d], lambda d=d: dr.at[d], lambda d=d: dr_r.at[d], at(dc=1))

    def mine(d):
        got(lambda: dr.at[d], lambda: dr_r.at[d])
        return scale * di[di_rows(d, core)] + dr[d].astype(F32)

    def return_images():
        for d in (2, 1, 3):
            sy[d - 1] = mine(d).astype(BF)
            put(lambda d=d: sy.at[d - 1], lambda d=d: dyr.at[d - 1], lambda d=d: dy_r.at[d - 1], at(dy=-d))

    def column(j, wrap):
        total = None
        for k in (1, 2, 3):
            term = xr[k - 1, pl.ds(j * HALF, HALF)].astype(F32)
            term = jnp.where(wraps[k] == wrap, term, 0.0)
            total = term if total is None else total + term
        return total

    def collect_x():
        for k in (1, 3, 2):
            got(lambda k=k: xr.at[k - 1], lambda k=k: xr_r.at[k - 1])
        sx[1] = (column(1, 0) + value(slot_at(0, 0, 1))).astype(BF)
        put(lambda: sx.at[1], lambda: o0.at[1], lambda: o0_r.at[1], at(dx=-2))
        for d in (1, 3):
            @pl.when(z > 0)
            def _():
                sx[d - 1] = column(d // 2, 1).astype(BF)

            put(lambda d=d: sx.at[d - 1], lambda d=d: o0.at[d - 1], lambda d=d: o0_r.at[d - 1], at(dx=-d), z > 0)

    def unnormalize(normed, norm, upstream):
        inner = jnp.sum(normed * upstream, axis=-1, keepdims=True)
        return (upstream - normed * inner) / norm

    for d in (1, 3, 2):
        send_image(d)
    along_z_high(2)
    along_z_high(1)
    along_z_high(3)
    for d in (1, 3):
        put_slot(own_low, 16 + d // 2, at(dx=d), z > 0)
    put_slot(own_low, slot_at(0, 0, 1), at(dx=2))
    along_z_low(2)
    put_slot(own_high, slot_at(0, 1, 1), at(dx=2))
    along_z_low(3)
    relay_image(0)
    relay_x(3)
    relay_z_near((3, 1, 2))
    relay_z_far((2, 1, 3))
    along_z_low(1)
    relay_image(1)
    relay_image(3)
    relay_x(2)
    relay_image(2)
    relay_x(1)
    got_chunk(0)
    for d in (0, 1, 3):
        got_image(d)
    early(0, True)
    got_chunk(3)
    early(3, False)
    got_chunk(2)
    early(2, False)
    got_image(2)
    late((2, 3), True)
    send_chunk(2)
    send_chunk(3)
    got_chunk(1)
    early(1, False)
    late((0, 1), False)
    send_chunk(0)
    send_chunk(1)
    swap_images()
    return_images()
    collect_z(2)
    collect_x()
    collect_z(1)
    collect_z(3)

    total = mine(0)
    for d in (1, 3, 2):
        got(lambda d=d: dyr.at[d - 1], lambda d=d: dy_r.at[d - 1])
        total = total + dyr[d - 1].astype(F32)
    grad_images[...] = unnormalize(inormed[...], inorm[...], total)

    lower = column(0, 0) + value(slot_at(0, 0, 0))
    got(lambda: o0.at[1], lambda: o0_r.at[1])
    lower = lower + o0[1].astype(F32)
    for d in (1, 3):
        got(lambda d=d: o0.at[d - 1], lambda d=d: o0_r.at[d - 1], z > 0)
        lower = lower + jnp.where(z > 0, o0[d - 1].astype(F32), 0.0)
    upper = value(slot_at(0, 1, 0))
    for k in (0, 1, 3, 2):
        got(lambda k=k: o1.at[k], lambda k=k: o1_r.at[k])
        upper = upper + o1[k].astype(F32)
    grad_texts[0:HALF] = unnormalize(tnormed[0:HALF], tnorm[0:HALF], lower)
    grad_texts[HALF:] = unnormalize(tnormed[HALF:], tnorm[HALF:], upper)

    for make, cond in pending:
        if cond is None:
            make().wait_send()
        else:
            @pl.when(cond)
            def _():
                make().wait_send()


def local(images, texts, logit_scale, bias):
    hbm = pl.BlockSpec(memory_space=pl.ANY)
    vmem = pl.BlockSpec(memory_space=pltpu.VMEM)
    smem = pl.BlockSpec(memory_space=pltpu.SMEM)
    dma = pltpu.SemaphoreType.DMA
    return pl.pallas_call(
        kernel,
        out_shape=[pltpu.VMEM((ROWS, WIDTH), F32)] * 2,
        in_specs=[smem, smem, hbm, hbm],
        out_specs=[vmem, vmem],
        scratch_shapes=[
            pltpu.VMEM((ROWS, WIDTH), BF),
            pltpu.VMEM((ROWS, WIDTH), BF),
            pltpu.VMEM((ROWS, WIDTH), F32),
            pltpu.VMEM((ROWS, WIDTH), F32),
            pltpu.VMEM((ROWS, 1), F32),
            pltpu.VMEM((ROWS, 1), F32),
            pltpu.VMEM((4, 2, ROWS, WIDTH), BF),
            pltpu.VMEM((21 * HALF, WIDTH), BF),
            pltpu.VMEM((8 * ROWS, WIDTH), F32),
            pltpu.VMEM((16 * HALF, WIDTH), F32),
            pltpu.VMEM((16 * HALF, WIDTH), BF),
            pltpu.VMEM((3, 2 * HALF, WIDTH), BF),
            pltpu.VMEM((3, 2, HALF, WIDTH), BF),
            pltpu.VMEM((3, HALF, WIDTH), BF),
            pltpu.VMEM((4, HALF, WIDTH), BF),
            pltpu.VMEM((4, ROWS, WIDTH), BF),
            pltpu.VMEM((3, ROWS, WIDTH), BF),
            pltpu.VMEM((3, HALF, WIDTH), BF),
            pltpu.VMEM((3, HALF, WIDTH), BF),
            pltpu.VMEM((4, ROWS, WIDTH), BF),
            pltpu.VMEM((3, ROWS, WIDTH), BF),
            dma((2,)),
            dma((64,)),
            dma((4, 2)),
            dma((21,)),
            dma((3,)),
            dma((3, 2)),
            dma((3,)),
            dma((4,)),
            dma((4,)),
            dma((3,)),
        ],
        compiler_params=pltpu.CompilerParams(
            collective_id=0, has_side_effects=True, vmem_limit_bytes=56 * 2**20
        ),
        name="pair_grads",
    )(logit_scale, bias, images, texts)


def solution(mesh):
    in_specs = (P(("loop", "group"), None), P(("loop", "group"), None), P(), P())
    out_specs = (P(("loop", "group"), None), P(("loop", "group"), None))
    return jax.shard_map(local, mesh=mesh, in_specs=in_specs, out_specs=out_specs, check_vma=False)
```

```python
import functools

import jax
import jax.numpy as jnp
from jax import lax
from jax.experimental import pallas as pl
from jax.experimental.pallas import tpu as pltpu
from jax.sharding import PartitionSpec as P

MESH = pl.DeviceIdType.MESH
ROWS = 128
HALF = 64
QUARTER = 32
WIDTH = 1152
BF = jnp.bfloat16
F32 = jnp.float32


CHUNK_AT = {2: 0, 3: 1, 0: 2, 1: 3}
IMAGE_AT = {0: 0, 1: 1, 3: 2, 2: 3}
EARLY = 6 * ROWS


def slot_at(k, h, j):
    return CHUNK_AT[k] * 4 + h * 2 + j


def kernel(
    logit_scale, bias, images_hbm, texts_hbm, grad_images, grad_texts,
    images, texts,
    inormed, tnormed, inorm, tnorm,
    im, tb, di, pt, pb,
    xr, zr, o0, o1, dr, dyr,
    sx, sz, sd, sy, sf, o2,
    o2_r, moved, send, im_h, im_r, tb_r, xr_r, zr_r, o0_r, o1_r, dr_r, dy_r,
):
    loop = lax.axis_index("loop")
    group = lax.axis_index("group")
    x = (group // 2) % 2 * 2 + loop // 4
    z = loop % 4
    y = group // 4
    core = group % 2

    def at(dx=0, dy=0, dz=0, dc=0):
        xx = (x + dx + 8) % 4
        yy = (y + dy + 4) % 4
        zz = (z + dz + 4) % 4
        return (xx % 2 * 4 + zz, yy * 4 + xx // 2 * 2 + (core + dc) % 2)

    barrier = pltpu.get_barrier_semaphore()
    partners = [at(dc=1)]
    for d in (1, 2, 3):
        partners += [at(dx=d), at(dy=d), at(dz=d)]
    for partner in partners:
        pl.semaphore_signal(barrier, inc=1, device_id=partner, device_id_type=MESH)

    loads = [
        pltpu.make_async_copy(texts_hbm, texts, moved.at[0]),
        pltpu.make_async_copy(images_hbm, images, moved.at[1]),
    ]
    for load in loads:
        load.start()

    def normalize(src, normed, norm):
        wide = src[...].astype(F32)
        n = jnp.sqrt(jnp.sum(wide * wide, axis=-1, keepdims=True) + 1e-06)
        out = wide / n
        normed[...] = out
        norm[...] = n
        return out.astype(BF)

    def part(ref, slot, count=1):
        return ref.at[pl.ds(pl.multiple_of(slot * HALF, HALF), HALF * count)]

    loads[0].wait()
    own_text = normalize(texts, tnormed, tnorm)
    part(tb, slot_at(0, 0, 0))[...] = own_text[0:HALF]
    part(tb, slot_at(0, 1, 0))[...] = own_text[HALF:]
    loads[1].wait()
    im[0, core] = normalize(images, inormed, inorm)

    pl.semaphore_wait(barrier, len(partners))

    pending = []
    numbers = iter(range(64))

    def put(src, dst, recv, device, cond=None):
        sem = send.at[next(numbers)]

        def make():
            return pltpu.make_async_remote_copy(
                src_ref=src(), dst_ref=dst(), send_sem=sem, recv_sem=recv(),
                device_id=device, device_id_type=MESH,
            )

        pending.append((make, cond))
        if cond is None:
            make().start()
        else:
            @pl.when(cond)
            def _():
                make().start()

    def drain(count):
        for make, cond in pending[:count]:
            if cond is None:
                make().wait_send()
            else:
                @pl.when(cond)
                def _():
                    make().wait_send()

        del pending[:count]

    def got(dst, recv, cond=None):
        def wait():
            pltpu.make_async_remote_copy(
                src_ref=dst(), dst_ref=dst(), send_sem=send.at[0], recv_sem=recv(),
                device_id=at(dc=1), device_id_type=MESH,
            ).wait_recv()

        if cond is None:
            wait()
        else:
            @pl.when(cond)
            def _():
                wait()

    def put_slot(src, dst, device, cond=None):
        put(lambda: part(tb, src), lambda: part(tb, dst), lambda: tb_r.at[dst], device, cond)

    def got_slot(slot, cond=None):
        got(lambda: part(tb, slot), lambda: tb_r.at[slot], cond)

    wraps = [(z + k >= 4).astype(jnp.int32) for k in range(4)]
    wrapped = [(z < k).astype(jnp.int32) for k in range(4)]

    own_low, own_high = slot_at(0, 0, 0), slot_at(0, 1, 0)

    def along_z_high(k):
        s = wraps[k]
        put_slot(own_high, s * (17 + k) + (1 - s) * slot_at(k, 1, 0), at(dz=k))

    def along_z_low(k):
        put_slot(own_low, slot_at(k, 0, 0), at(dz=k), wraps[k] == 0)

    def relay_z_near(d, order):
        got_slot(16 + d // 2, z > 0)
        for k in order:
            put_slot(16 + d // 2, slot_at(k, 0, d // 2), at(dz=k), wraps[k] == 1)

    def relay_z_far(order):
        got_slot(slot_at(0, 0, 1))
        for k in order:
            put_slot(slot_at(0, 0, 1), slot_at(k, 0, 1), at(dz=k), wraps[k] == 0)

    def relay_x(k):
        s = wrapped[k]
        here = s * (17 + k) + (1 - s) * slot_at(k, 1, 0)
        got_slot(here)
        put_slot(here, slot_at(k, 1, 1), at(dx=s + 2))
        put_slot(here, slot_at(k, 1, 0), at(dx=1), s == 1)

    def send_image(d, h):
        a = IMAGE_AT[d]
        rows = pl.ds(h * HALF, HALF)
        put(lambda: im.at[0, core, rows], lambda: im.at[a, core, rows], lambda: im_h.at[a, h], at(dy=d))

    def forward_image(d):
        a, b = IMAGE_AT[d], IMAGE_AT[2]
        h = d // 2
        rows = pl.ds(h * HALF, HALF)
        got(lambda: im.at[a, core, rows], lambda: im_h.at[a, h])
        put(lambda: im.at[a, core, rows], lambda: im.at[b, core, rows], lambda: im_h.at[b, h], at(dy=d))

    def relay_image(d):
        a = IMAGE_AT[d]
        for h in (0, 1):
            if d == 2 or d and h != d // 2:
                rows = pl.ds(h * HALF, HALF)
                got(lambda: im.at[a, core, rows], lambda: im_h.at[a, h])
        put(lambda: im.at[a, core], lambda: im.at[a, core], lambda: im_r.at[a], at(dc=1))

    def got_image(d):
        a = IMAGE_AT[d]
        got(lambda: im.at[a, 1 - core], lambda: im_r.at[a])

    scale = logit_scale[0]
    shift = bias[0]

    def early(k, first):
        base = CHUNK_AT[k] * 4 * HALF
        rows = pl.ds(base, 4 * HALF)
        t = tb[rows]
        i = im[0:3].reshape(EARLY, WIDTH)
        logits = scale * lax.dot_general(t, i, (((1,), (1,)), ((), ())), preferred_element_type=F32) + shift
        if k == 0:
            r = lax.broadcasted_iota(jnp.int32, logits.shape, 0)
            c = lax.broadcasted_iota(jnp.int32, logits.shape, 1)
            own = r // (2 * HALF) * HALF + r % HALF + core * ROWS
            positive = (c == own) & (r // HALF % 2 == 0)
            signs = jnp.where(positive, 1.0, -1.0).astype(F32)
            slopes = -signs / (1.0 + jnp.exp(signs * logits))
        else:
            slopes = 1.0 / (1.0 + jnp.exp(-logits))
        slopes = slopes.astype(BF)
        pt[rows] = jnp.dot(slopes, i, preferred_element_type=F32)
        term = lax.dot_general(slopes, t, (((0,), (0,)), ((), ())), preferred_element_type=F32)
        if first:
            di[0:EARLY] = term
        else:
            di[0:EARLY] += term

    def late(ks, first):
        rows = pl.ds(CHUNK_AT[ks[0]] * 4 * HALF, 4 * HALF * len(ks))
        t = tb[rows]
        i = im[3].reshape(2 * ROWS, WIDTH)
        logits = scale * lax.dot_general(i, t, (((1,), (1,)), ((), ())), preferred_element_type=F32) + shift
        slopes = (1.0 / (1.0 + jnp.exp(-logits))).astype(BF)
        term = lax.dot_general(slopes, i, (((0,), (0,)), ((), ())), preferred_element_type=F32)
        pb[rows] = (scale * (pt[rows] + term)).astype(BF)
        term = jnp.dot(slopes, t, preferred_element_type=F32)
        if first:
            di[EARLY:] = term
        else:
            di[EARLY:] += term

    def value(slot):
        return part(pb, slot)[...].astype(F32)

    def got_chunk(k):
        if k == 0:
            got_slot(slot_at(0, 1, 1))
            return
        got_slot(slot_at(k, 0, 0))
        got_slot(slot_at(k, 0, 1))
        got_slot(slot_at(k, 1, 0), wrapped[k] == 1)
        got_slot(slot_at(k, 1, 1))

    def send_chunk(k, order):
        if k == 0:
            put(lambda: part(pb, slot_at(0, 1, 1)), lambda: o1.at[0], lambda: o1_r.at[0], at(dx=2))
            return
        s = wrapped[k]
        for which in order:
            if which == "1":
                put(lambda: part(pb, slot_at(k, 1, 1)), lambda: zr.at[k - 1, 1], lambda: zr_r.at[k - 1, 1], at(dx=-s - 2))
            elif which == "0":
                put(lambda: part(pb, slot_at(k, 1, 0)), lambda: zr.at[k - 1, 0], lambda: zr_r.at[k - 1, 0], at(dx=-1), s == 1)
            else:
                put(lambda: part(pb, slot_at(k, 0, 0), 2), lambda: xr.at[k - 1], lambda: xr_r.at[k - 1], at(dz=-k))

    def collect_z(k):
        s = wrapped[k]
        got(lambda: zr.at[k - 1, 1], lambda: zr_r.at[k - 1, 1])
        got(lambda: zr.at[k - 1, 0], lambda: zr_r.at[k - 1, 0], s == 1)

        @pl.when(s == 1)
        def _():
            sf[...] = zr[k - 1, 1].astype(F32) + zr[k - 1, 0].astype(F32)

        @pl.when(s == 0)
        def _():
            sf[...] = zr[k - 1, 1].astype(F32) + value(slot_at(k, 1, 0))

        if k == 2:
            sz[k - 1] = sf[...].astype(BF)
            for h, d in ((0, 3), (1, 1)):
                rows = pl.ds(h * QUARTER, QUARTER)
                put(lambda rows=rows: sz.at[1, rows], lambda h=h: o2.at[h], lambda h=h: o2_r.at[h], at(dz=d))
            return
        h = k // 2
        rows = pl.ds(h * QUARTER, QUARTER)
        got(lambda: o2.at[h], lambda: o2_r.at[h])
        sf[rows] += o2[h].astype(F32)
        sz[k - 1] = sf[...].astype(BF)
        put(lambda: sz.at[k - 1], lambda: o1.at[k], lambda: o1_r.at[k], at(dz=-k))

    def di_rows(d, half):
        return pl.ds(pl.multiple_of(IMAGE_AT[d] * 2 * ROWS + half * ROWS, ROWS), ROWS)

    def swap_images():
        for d in (2, 1, 3, 0):
            sd[d] = (scale * di[di_rows(d, 1 - core)]).astype(BF)
            put(lambda d=d: sd.at[d], lambda d=d: dr.at[d], lambda d=d: dr_r.at[d], at(dc=1))

    def mine(d):
        got(lambda: dr.at[d], lambda: dr_r.at[d])
        return scale * di[di_rows(d, core)] + dr[d].astype(F32)

    def return_images():
        for d in (2, 1, 3):
            sy[d - 1] = mine(d).astype(BF)
            put(lambda d=d: sy.at[d - 1], lambda d=d: dyr.at[d - 1], lambda d=d: dy_r.at[d - 1], at(dy=-d))

    def column(j, wrap):
        total = None
        for k in (1, 2, 3):
            term = xr[k - 1, pl.ds(j * HALF, HALF)].astype(F32)
            term = jnp.where(wraps[k] == wrap, term, 0.0)
            total = term if total is None else total + term
        return total

    def got_column():
        for k in (1, 3, 2):
            got(lambda k=k: xr.at[k - 1], lambda k=k: xr_r.at[k - 1])

    def collect_far():
        sx[1] = (column(1, 0) + value(slot_at(0, 0, 1))).astype(BF)
        put(lambda: sx.at[1], lambda: o0.at[1], lambda: o0_r.at[1], at(dx=-2))

    def collect_near():
        for d in (1, 3):
            @pl.when(z > 0)
            def _():
                sx[d - 1] = column(d // 2, 1).astype(BF)

            put(lambda d=d: sx.at[d - 1], lambda d=d: o0.at[d - 1], lambda d=d: o0_r.at[d - 1], at(dx=-d), z > 0)

    def unnormalize(normed, norm, upstream):
        inner = jnp.sum(normed * upstream, axis=-1, keepdims=True)
        return (upstream - normed * inner) / norm

    for d, h in ((1, 0), (3, 1), (1, 1), (3, 0)):
        send_image(d, h)
    along_z_high(2)
    along_z_high(1)
    along_z_high(3)
    put_slot(own_low, 16, at(dx=1), z > 0)
    put_slot(own_low, 17, at(dx=3), z > 0)
    put_slot(own_low, slot_at(0, 0, 1), at(dx=2))
    along_z_low(2)
    put_slot(own_high, slot_at(0, 1, 1), at(dx=2))
    along_z_low(3)
    relay_image(0)
    relay_x(3)
    relay_z_near(1, (3, 1, 2))
    relay_z_near(3, (3, 1, 2))
    relay_z_far((2, 1, 3))
    along_z_low(1)
    forward_image(1)
    forward_image(3)
    relay_image(1)
    relay_image(3)
    relay_x(2)
    relay_image(2)
    relay_x(1)
    got_chunk(0)
    for d in (0, 1, 3):
        got_image(d)
    early(0, True)
    got_chunk(3)
    early(3, False)
    got_chunk(2)
    early(2, False)
    inbound = len(pending)
    got_image(2)
    late((2, 3), True)
    send_chunk(2, "10x")
    send_chunk(3, "10x")
    got_chunk(1)
    early(1, False)
    late((0, 1), False)
    send_chunk(0, "10x")
    send_chunk(1, "10x")
    swap_images()
    return_images()
    collect_z(2)
    got_column()
    collect_far()
    collect_near()
    collect_z(1)
    collect_z(3)

    total = mine(0)
    for d in (1, 3, 2):
        got(lambda d=d: dyr.at[d - 1], lambda d=d: dy_r.at[d - 1])
        total = total + dyr[d - 1].astype(F32)
    grad_images[...] = unnormalize(inormed[...], inorm[...], total)

    lower = column(0, 0) + value(slot_at(0, 0, 0))
    got(lambda: o0.at[1], lambda: o0_r.at[1])
    lower = lower + o0[1].astype(F32)
    for d in (1, 3):
        got(lambda d=d: o0.at[d - 1], lambda d=d: o0_r.at[d - 1], z > 0)
        lower = lower + jnp.where(z > 0, o0[d - 1].astype(F32), 0.0)
    upper = value(slot_at(0, 1, 0))
    for k in (0, 1, 3):
        got(lambda k=k: o1.at[k], lambda k=k: o1_r.at[k])
        upper = upper + o1[k].astype(F32)
    grad_texts[0:HALF] = unnormalize(tnormed[0:HALF], tnorm[0:HALF], lower)
    grad_texts[HALF:] = unnormalize(tnormed[HALF:], tnorm[HALF:], upper)

    drain(len(pending))


def local(images, texts, logit_scale, bias):
    hbm = pl.BlockSpec(memory_space=pl.ANY)
    vmem = pl.BlockSpec(memory_space=pltpu.VMEM)
    smem = pl.BlockSpec(memory_space=pltpu.SMEM)
    dma = pltpu.SemaphoreType.DMA
    return pl.pallas_call(
        kernel,
        out_shape=[pltpu.VMEM((ROWS, WIDTH), F32)] * 2,
        in_specs=[smem, smem, hbm, hbm],
        out_specs=[vmem, vmem],
        scratch_shapes=[
            pltpu.VMEM((ROWS, WIDTH), BF),
            pltpu.VMEM((ROWS, WIDTH), BF),
            pltpu.VMEM((ROWS, WIDTH), F32),
            pltpu.VMEM((ROWS, WIDTH), F32),
            pltpu.VMEM((ROWS, 1), F32),
            pltpu.VMEM((ROWS, 1), F32),
            pltpu.VMEM((4, 2, ROWS, WIDTH), BF),
            pltpu.VMEM((21 * HALF, WIDTH), BF),
            pltpu.VMEM((8 * ROWS, WIDTH), F32),
            pltpu.VMEM((16 * HALF, WIDTH), F32),
            pltpu.VMEM((16 * HALF, WIDTH), BF),
            pltpu.VMEM((3, 2 * HALF, WIDTH), BF),
            pltpu.VMEM((3, 2, HALF, WIDTH), BF),
            pltpu.VMEM((3, HALF, WIDTH), BF),
            pltpu.VMEM((4, HALF, WIDTH), BF),
            pltpu.VMEM((4, ROWS, WIDTH), BF),
            pltpu.VMEM((3, ROWS, WIDTH), BF),
            pltpu.VMEM((3, HALF, WIDTH), BF),
            pltpu.VMEM((3, HALF, WIDTH), BF),
            pltpu.VMEM((4, ROWS, WIDTH), BF),
            pltpu.VMEM((3, ROWS, WIDTH), BF),
            pltpu.VMEM((HALF, WIDTH), F32),
            pltpu.VMEM((2, QUARTER, WIDTH), BF),
            dma((2,)),
            dma((2,)),
            dma((64,)),
            dma((4, 2)),
            dma((4,)),
            dma((21,)),
            dma((3,)),
            dma((3, 2)),
            dma((3,)),
            dma((4,)),
            dma((4,)),
            dma((3,)),
        ],
        compiler_params=pltpu.CompilerParams(
            collective_id=0, has_side_effects=True, vmem_limit_bytes=56 * 2**20
        ),
        name="pair_grads",
    )(logit_scale, bias, images, texts)


def solution(mesh):
    in_specs = (P(("loop", "group"), None), P(("loop", "group"), None), P(), P())
    out_specs = (P(("loop", "group"), None), P(("loop", "group"), None))
    return jax.shard_map(local, mesh=mesh, in_specs=in_specs, out_specs=out_specs, check_vma=False)
```

```python
import functools

import jax
import jax.numpy as jnp
from jax import lax
from jax.experimental import pallas as pl
from jax.experimental.pallas import tpu as pltpu
from jax.sharding import PartitionSpec as P

MESH = pl.DeviceIdType.MESH
ROWS = 128
HALF = 64
QUARTER = 32
WIDTH = 1152
BF = jnp.bfloat16
F32 = jnp.float32


CHUNK_AT = {2: 0, 3: 1, 0: 2, 1: 3}
IMAGE_AT = {0: 0, 1: 1, 3: 2, 2: 3}
EARLY = 6 * ROWS


def slot_at(k, h, j):
    return CHUNK_AT[k] * 4 + h * 2 + j


def kernel(
    logit_scale, bias, images_hbm, texts_hbm, grad_images, grad_texts,
    images, texts,
    inormed, tnormed, inorm, tnorm,
    im, tb, di, pt, pb,
    xr, zr, o0, o1, dr, dyr,
    sx, sz, sd, sy, sf, o2, de, dl,
    o2_r, moved, send, im_h, im_r, tb_r, xr_r, zr_r, o0_r, o1_r, dr_r, dy_r,
):
    loop = lax.axis_index("loop")
    group = lax.axis_index("group")
    x = (group // 2) % 2 * 2 + loop // 4
    z = loop % 4
    y = group // 4
    core = group % 2

    def at(dx=0, dy=0, dz=0, dc=0):
        xx = (x + dx + 8) % 4
        yy = (y + dy + 4) % 4
        zz = (z + dz + 4) % 4
        return (xx % 2 * 4 + zz, yy * 4 + xx // 2 * 2 + (core + dc) % 2)

    barrier = pltpu.get_barrier_semaphore()
    partners = [at(dc=1)]
    for d in (1, 2, 3):
        partners += [at(dx=d), at(dy=d), at(dz=d)]
    for partner in partners:
        pl.semaphore_signal(barrier, inc=1, device_id=partner, device_id_type=MESH)

    loads = [
        pltpu.make_async_copy(texts_hbm, texts, moved.at[0]),
        pltpu.make_async_copy(images_hbm, images, moved.at[1]),
    ]
    for load in loads:
        load.start()

    def normalize(src, normed, norm):
        wide = src[...].astype(F32)
        n = jnp.sqrt(jnp.sum(wide * wide, axis=-1, keepdims=True) + 1e-06)
        out = wide / n
        normed[...] = out
        norm[...] = n
        return out.astype(BF)

    def part(ref, slot, count=1):
        return ref.at[pl.ds(pl.multiple_of(slot * HALF, HALF), HALF * count)]

    loads[0].wait()
    own_text = normalize(texts, tnormed, tnorm)
    part(tb, slot_at(0, 0, 0))[...] = own_text[0:HALF]
    part(tb, slot_at(0, 1, 0))[...] = own_text[HALF:]
    loads[1].wait()
    im[0, core] = normalize(images, inormed, inorm)

    pl.semaphore_wait(barrier, len(partners))

    pending = []
    numbers = iter(range(64))

    def put(src, dst, recv, device, cond=None):
        sem = send.at[next(numbers)]

        def make():
            return pltpu.make_async_remote_copy(
                src_ref=src(), dst_ref=dst(), send_sem=sem, recv_sem=recv(),
                device_id=device, device_id_type=MESH,
            )

        pending.append((make, cond))
        if cond is None:
            make().start()
        else:
            @pl.when(cond)
            def _():
                make().start()

    def drain(count):
        for make, cond in pending[:count]:
            if cond is None:
                make().wait_send()
            else:
                @pl.when(cond)
                def _():
                    make().wait_send()

        del pending[:count]

    def got(dst, recv, cond=None):
        def wait():
            pltpu.make_async_remote_copy(
                src_ref=dst(), dst_ref=dst(), send_sem=send.at[0], recv_sem=recv(),
                device_id=at(dc=1), device_id_type=MESH,
            ).wait_recv()

        if cond is None:
            wait()
        else:
            @pl.when(cond)
            def _():
                wait()

    def put_slot(src, dst, device, cond=None):
        put(lambda: part(tb, src), lambda: part(tb, dst), lambda: tb_r.at[dst], device, cond)

    def got_slot(slot, cond=None):
        got(lambda: part(tb, slot), lambda: tb_r.at[slot], cond)

    wraps = [(z + k >= 4).astype(jnp.int32) for k in range(4)]
    wrapped = [(z < k).astype(jnp.int32) for k in range(4)]

    own_low, own_high = slot_at(0, 0, 0), slot_at(0, 1, 0)

    def along_z_high(k):
        s = wraps[k]
        put_slot(own_high, s * (17 + k) + (1 - s) * slot_at(k, 1, 0), at(dz=k))

    def along_z_low(k):
        put_slot(own_low, slot_at(k, 0, 0), at(dz=k), wraps[k] == 0)

    def relay_z_near(d, order):
        got_slot(16 + d // 2, z > 0)
        for k in order:
            put_slot(16 + d // 2, slot_at(k, 0, d // 2), at(dz=k), wraps[k] == 1)

    def relay_z_far(order):
        got_slot(slot_at(0, 0, 1))
        for k in order:
            put_slot(slot_at(0, 0, 1), slot_at(k, 0, 1), at(dz=k), wraps[k] == 0)

    def relay_x(k):
        s = wrapped[k]
        here = s * (17 + k) + (1 - s) * slot_at(k, 1, 0)
        got_slot(here)
        put_slot(here, slot_at(k, 1, 1), at(dx=s + 2))
        put_slot(here, slot_at(k, 1, 0), at(dx=1), s == 1)

    def send_image(d, h):
        a = IMAGE_AT[d]
        rows = pl.ds(h * HALF, HALF)
        put(lambda: im.at[0, core, rows], lambda: im.at[a, core, rows], lambda: im_h.at[a, h], at(dy=d))

    def forward_image(d):
        a, b = IMAGE_AT[d], IMAGE_AT[2]
        h = d // 2
        rows = pl.ds(h * HALF, HALF)
        got(lambda: im.at[a, core, rows], lambda: im_h.at[a, h])
        put(lambda: im.at[a, core, rows], lambda: im.at[b, core, rows], lambda: im_h.at[b, h], at(dy=d))

    def relay_image(d):
        a = IMAGE_AT[d]
        for h in (0, 1):
            if d == 2 or d and h != d // 2:
                rows = pl.ds(h * HALF, HALF)
                got(lambda: im.at[a, core, rows], lambda: im_h.at[a, h])
        put(lambda: im.at[a, core], lambda: im.at[a, core], lambda: im_r.at[a], at(dc=1))

    def got_image(d):
        a = IMAGE_AT[d]
        got(lambda: im.at[a, 1 - core], lambda: im_r.at[a])

    scale = logit_scale[0]
    shift = bias[0]

    def early(k, first):
        base = CHUNK_AT[k] * 4 * HALF
        rows = pl.ds(base, 4 * HALF)
        t = tb[rows]
        i = im[0:3].reshape(EARLY, WIDTH)
        logits = scale * lax.dot_general(t, i, (((1,), (1,)), ((), ())), preferred_element_type=F32) + shift
        if k == 0:
            r = lax.broadcasted_iota(jnp.int32, logits.shape, 0)
            c = lax.broadcasted_iota(jnp.int32, logits.shape, 1)
            own = r // (2 * HALF) * HALF + r % HALF + core * ROWS
            positive = (c == own) & (r // HALF % 2 == 0)
            signs = jnp.where(positive, 1.0, -1.0).astype(F32)
            slopes = -signs / (1.0 + jnp.exp(signs * logits))
        else:
            slopes = 1.0 / (1.0 + jnp.exp(-logits))
        slopes = slopes.astype(BF)
        pt[rows] = jnp.dot(slopes, i, preferred_element_type=F32)
        term = lax.dot_general(slopes, t, (((0,), (0,)), ((), ())), preferred_element_type=F32)
        if first:
            di[0:EARLY] = term
        else:
            di[0:EARLY] += term

    def early_images(k):
        rows = pl.ds(CHUNK_AT[k] * 4 * HALF, 4 * HALF)
        t = tb[rows]
        i = im[0:3].reshape(EARLY, WIDTH)
        logits = scale * lax.dot_general(t, i, (((1,), (1,)), ((), ())), preferred_element_type=F32) + shift
        slopes = (1.0 / (1.0 + jnp.exp(-logits))).astype(BF)
        de[...] = slopes
        di[0:EARLY] += lax.dot_general(slopes, t, (((0,), (0,)), ((), ())), preferred_element_type=F32)

    def early_texts(k):
        rows = pl.ds(CHUNK_AT[k] * 4 * HALF, 4 * HALF)
        pt[rows] = jnp.dot(de[...], im[0:3].reshape(EARLY, WIDTH), preferred_element_type=F32)

    def late_images(ks):
        rows = pl.ds(CHUNK_AT[ks[0]] * 4 * HALF, 4 * HALF * len(ks))
        t = tb[rows]
        i = im[3].reshape(2 * ROWS, WIDTH)
        logits = scale * lax.dot_general(i, t, (((1,), (1,)), ((), ())), preferred_element_type=F32) + shift
        slopes = (1.0 / (1.0 + jnp.exp(-logits))).astype(BF)
        dl[...] = slopes
        di[EARLY:] += jnp.dot(slopes, t, preferred_element_type=F32)

    def late_texts(ks):
        rows = pl.ds(CHUNK_AT[ks[0]] * 4 * HALF, 4 * HALF * len(ks))
        i = im[3].reshape(2 * ROWS, WIDTH)
        term = lax.dot_general(dl[...], i, (((0,), (0,)), ((), ())), preferred_element_type=F32)
        pb[rows] = (pt[rows] + term).astype(BF)

    def late(ks, first):
        rows = pl.ds(CHUNK_AT[ks[0]] * 4 * HALF, 4 * HALF * len(ks))
        t = tb[rows]
        i = im[3].reshape(2 * ROWS, WIDTH)
        logits = scale * lax.dot_general(i, t, (((1,), (1,)), ((), ())), preferred_element_type=F32) + shift
        slopes = (1.0 / (1.0 + jnp.exp(-logits))).astype(BF)
        term = lax.dot_general(slopes, i, (((0,), (0,)), ((), ())), preferred_element_type=F32)
        pb[rows] = (pt[rows] + term).astype(BF)
        term = jnp.dot(slopes, t, preferred_element_type=F32)
        if first:
            di[EARLY:] = term
        else:
            di[EARLY:] += term

    def value(slot):
        return part(pb, slot)[...].astype(F32)

    def got_chunk(k):
        if k == 0:
            got_slot(slot_at(0, 1, 1))
            return
        got_slot(slot_at(k, 0, 0))
        got_slot(slot_at(k, 0, 1))
        got_slot(slot_at(k, 1, 0), wrapped[k] == 1)
        got_slot(slot_at(k, 1, 1))

    def send_chunk(k, order):
        if k == 0:
            put(lambda: part(pb, slot_at(0, 1, 1)), lambda: o1.at[0], lambda: o1_r.at[0], at(dx=2))
            return
        s = wrapped[k]
        for which in order:
            if which == "1":
                put(lambda: part(pb, slot_at(k, 1, 1)), lambda: zr.at[k - 1, 1], lambda: zr_r.at[k - 1, 1], at(dx=-s - 2))
            elif which == "0":
                put(lambda: part(pb, slot_at(k, 1, 0)), lambda: zr.at[k - 1, 0], lambda: zr_r.at[k - 1, 0], at(dx=-1), s == 1)
            else:
                put(lambda: part(pb, slot_at(k, 0, 0), 2), lambda: xr.at[k - 1], lambda: xr_r.at[k - 1], at(dz=-k))

    def collect_z(k):
        s = wrapped[k]
        got(lambda: zr.at[k - 1, 1], lambda: zr_r.at[k - 1, 1])
        got(lambda: zr.at[k - 1, 0], lambda: zr_r.at[k - 1, 0], s == 1)

        @pl.when(s == 1)
        def _():
            sf[...] = zr[k - 1, 1].astype(F32) + zr[k - 1, 0].astype(F32)

        @pl.when(s == 0)
        def _():
            sf[...] = zr[k - 1, 1].astype(F32) + value(slot_at(k, 1, 0))

        if k == 2:
            sz[k - 1] = sf[...].astype(BF)
            for h, d in ((0, 3), (1, 1)):
                rows = pl.ds(h * QUARTER, QUARTER)
                put(lambda rows=rows: sz.at[1, rows], lambda h=h: o2.at[h], lambda h=h: o2_r.at[h], at(dz=d))
            return
        h = k // 2
        rows = pl.ds(h * QUARTER, QUARTER)
        got(lambda: o2.at[h], lambda: o2_r.at[h])
        sf[rows] += o2[h].astype(F32)
        sz[k - 1] = sf[...].astype(BF)
        put(lambda: sz.at[k - 1], lambda: o1.at[k], lambda: o1_r.at[k], at(dz=-k))

    def di_rows(d, half):
        return pl.ds(pl.multiple_of(IMAGE_AT[d] * 2 * ROWS + half * ROWS, ROWS), ROWS)

    def swap_image(d):
        sd[d] = di[di_rows(d, 1 - core)].astype(BF)
        put(lambda: sd.at[d], lambda: dr.at[d], lambda: dr_r.at[d], at(dc=1))

    def return_image(d):
        sy[d - 1] = mine(d).astype(BF)
        put(lambda: sy.at[d - 1], lambda: dyr.at[d - 1], lambda: dy_r.at[d - 1], at(dy=-d))

    def mine(d):
        got(lambda: dr.at[d], lambda: dr_r.at[d])
        return di[di_rows(d, core)] + dr[d].astype(F32)

    def return_images():
        for d in (2, 1, 3):
            sy[d - 1] = mine(d).astype(BF)
            put(lambda d=d: sy.at[d - 1], lambda d=d: dyr.at[d - 1], lambda d=d: dy_r.at[d - 1], at(dy=-d))

    def column(j, wrap):
        total = None
        for k in (1, 2, 3):
            term = xr[k - 1, pl.ds(j * HALF, HALF)].astype(F32)
            term = jnp.where(wraps[k] == wrap, term, 0.0)
            total = term if total is None else total + term
        return total

    def got_column():
        for k in (1, 3, 2):
            got(lambda k=k: xr.at[k - 1], lambda k=k: xr_r.at[k - 1])

    def collect_far():
        sx[1] = (column(1, 0) + value(slot_at(0, 0, 1))).astype(BF)
        put(lambda: sx.at[1], lambda: o0.at[1], lambda: o0_r.at[1], at(dx=-2))

    def collect_near():
        for d in (1, 3):
            @pl.when(z > 0)
            def _():
                sx[d - 1] = column(d // 2, 1).astype(BF)

            put(lambda d=d: sx.at[d - 1], lambda d=d: o0.at[d - 1], lambda d=d: o0_r.at[d - 1], at(dx=-d), z > 0)

    def unnormalize(normed, norm, upstream):
        inner = jnp.sum(normed * upstream, axis=-1, keepdims=True)
        return (upstream - normed * inner) / norm

    for d, h in ((1, 0), (3, 1), (1, 1), (3, 0)):
        send_image(d, h)
    along_z_high(2)
    along_z_high(1)
    along_z_high(3)
    put_slot(own_low, 16, at(dx=1), z > 0)
    put_slot(own_low, 17, at(dx=3), z > 0)
    put_slot(own_low, slot_at(0, 0, 1), at(dx=2))
    along_z_low(2)
    put_slot(own_high, slot_at(0, 1, 1), at(dx=2))
    along_z_low(3)
    relay_image(0)
    relay_x(3)
    relay_z_near(1, (3, 1, 2))
    relay_z_near(3, (3, 1, 2))
    relay_z_far((2, 1, 3))
    along_z_low(1)
    forward_image(1)
    forward_image(3)
    relay_image(1)
    relay_image(3)
    relay_x(2)
    relay_image(2)
    relay_x(1)
    got_chunk(0)
    for d in (0, 1, 3):
        got_image(d)
    early(0, True)
    got_chunk(3)
    early(3, False)
    got_chunk(2)
    early(2, False)
    inbound = len(pending)
    got_image(2)
    late((2, 3), True)
    send_chunk(2, "10x")
    send_chunk(3, "10x")
    got_chunk(1)
    late_images((0, 1))
    swap_image(2)
    early_images(1)
    for d in (1, 3, 0):
        swap_image(d)
    early_texts(1)
    late_texts((0, 1))
    send_chunk(0, "10x")
    send_chunk(1, "10x")
    return_images()
    collect_z(2)
    got_column()
    collect_far()
    collect_near()
    collect_z(1)
    collect_z(3)

    total = mine(0)
    for d in (1, 3, 2):
        got(lambda d=d: dyr.at[d - 1], lambda d=d: dy_r.at[d - 1])
        total = total + dyr[d - 1].astype(F32)
    grad_images[...] = unnormalize(inormed[...], inorm[...], total)

    lower = column(0, 0) + value(slot_at(0, 0, 0))
    got(lambda: o0.at[1], lambda: o0_r.at[1])
    lower = lower + o0[1].astype(F32)
    for d in (1, 3):
        got(lambda d=d: o0.at[d - 1], lambda d=d: o0_r.at[d - 1], z > 0)
        lower = lower + jnp.where(z > 0, o0[d - 1].astype(F32), 0.0)
    upper = value(slot_at(0, 1, 0))
    for k in (0, 1, 3):
        got(lambda k=k: o1.at[k], lambda k=k: o1_r.at[k])
        upper = upper + o1[k].astype(F32)
    grad_texts[0:HALF] = unnormalize(tnormed[0:HALF], tnorm[0:HALF], lower)
    grad_texts[HALF:] = unnormalize(tnormed[HALF:], tnorm[HALF:], upper)

    drain(len(pending))


def local(images, texts, logit_scale, bias):
    hbm = pl.BlockSpec(memory_space=pl.ANY)
    vmem = pl.BlockSpec(memory_space=pltpu.VMEM)
    smem = pl.BlockSpec(memory_space=pltpu.SMEM)
    dma = pltpu.SemaphoreType.DMA
    grads = pl.pallas_call(
        kernel,
        out_shape=[pltpu.VMEM((ROWS, WIDTH), F32)] * 2,
        in_specs=[smem, smem, hbm, hbm],
        out_specs=[vmem, vmem],
        scratch_shapes=[
            pltpu.VMEM((ROWS, WIDTH), BF),
            pltpu.VMEM((ROWS, WIDTH), BF),
            pltpu.VMEM((ROWS, WIDTH), F32),
            pltpu.VMEM((ROWS, WIDTH), F32),
            pltpu.VMEM((ROWS, 1), F32),
            pltpu.VMEM((ROWS, 1), F32),
            pltpu.VMEM((4, 2, ROWS, WIDTH), BF),
            pltpu.VMEM((21 * HALF, WIDTH), BF),
            pltpu.VMEM((8 * ROWS, WIDTH), F32),
            pltpu.VMEM((16 * HALF, WIDTH), F32),
            pltpu.VMEM((16 * HALF, WIDTH), BF),
            pltpu.VMEM((3, 2 * HALF, WIDTH), BF),
            pltpu.VMEM((3, 2, HALF, WIDTH), BF),
            pltpu.VMEM((3, HALF, WIDTH), BF),
            pltpu.VMEM((4, HALF, WIDTH), BF),
            pltpu.VMEM((4, ROWS, WIDTH), BF),
            pltpu.VMEM((3, ROWS, WIDTH), BF),
            pltpu.VMEM((3, HALF, WIDTH), BF),
            pltpu.VMEM((3, HALF, WIDTH), BF),
            pltpu.VMEM((4, ROWS, WIDTH), BF),
            pltpu.VMEM((3, ROWS, WIDTH), BF),
            pltpu.VMEM((HALF, WIDTH), F32),
            pltpu.VMEM((2, QUARTER, WIDTH), BF),
            pltpu.VMEM((4 * HALF, EARLY), BF),
            pltpu.VMEM((2 * ROWS, 8 * HALF), BF),
            dma((2,)),
            dma((2,)),
            dma((64,)),
            dma((4, 2)),
            dma((4,)),
            dma((21,)),
            dma((3,)),
            dma((3, 2)),
            dma((3,)),
            dma((4,)),
            dma((4,)),
            dma((3,)),
        ],
        compiler_params=pltpu.CompilerParams(
            collective_id=0, has_side_effects=True, vmem_limit_bytes=56 * 2**20
        ),
        name="pair_grads",
    )(logit_scale, bias, images, texts)
    return tuple(logit_scale[0] * grad for grad in grads)


def solution(mesh):
    in_specs = (P(("loop", "group"), None), P(("loop", "group"), None), P(), P())
    out_specs = (P(("loop", "group"), None), P(("loop", "group"), None))
    return jax.shard_map(local, mesh=mesh, in_specs=in_specs, out_specs=out_specs, check_vma=False)
```

```python
import functools

import jax
import jax.numpy as jnp
from jax import lax
from jax.experimental import pallas as pl
from jax.experimental.pallas import tpu as pltpu
from jax.sharding import PartitionSpec as P

MESH = pl.DeviceIdType.MESH
ROWS = 128
HALF = 64
QUARTER = 32
WIDTH = 1152
BF = jnp.bfloat16
F32 = jnp.float32


CHUNK_AT = {2: 0, 3: 1, 0: 2, 1: 3}
IMAGE_AT = {0: 0, 1: 1, 3: 2, 2: 3}
EARLY = 6 * ROWS


def slot_at(k, h, j):
    return CHUNK_AT[k] * 4 + h * 2 + j


def kernel(
    logit_scale, bias, images_hbm, texts_hbm, grad_images, grad_texts,
    images, texts,
    inormed, tnormed, inorm, tnorm,
    im, tb, di, pt, pb,
    xr, zr, o0, o1, dr, dyr,
    sx, sz, sd, sy, sf, o2, de, dl, y2, sm,
    o2_r, y2_r, moved, send, im_h, im_r, tb_r, xr_r, zr_r, o0_r, o1_r, dr_r, dy_r,
):
    loop = lax.axis_index("loop")
    group = lax.axis_index("group")
    x = (group // 2) % 2 * 2 + loop // 4
    z = loop % 4
    y = group // 4
    core = group % 2

    def at(dx=0, dy=0, dz=0, dc=0):
        xx = (x + dx + 8) % 4
        yy = (y + dy + 4) % 4
        zz = (z + dz + 4) % 4
        return (xx % 2 * 4 + zz, yy * 4 + xx // 2 * 2 + (core + dc) % 2)

    barrier = pltpu.get_barrier_semaphore()
    partners = [at(dc=1)]
    for d in (1, 2, 3):
        partners += [at(dx=d), at(dy=d), at(dz=d)]
    for partner in partners:
        pl.semaphore_signal(barrier, inc=1, device_id=partner, device_id_type=MESH)

    loads = [
        pltpu.make_async_copy(texts_hbm, texts, moved.at[0]),
        pltpu.make_async_copy(images_hbm, images, moved.at[1]),
    ]
    for load in loads:
        load.start()

    def normalize(src, normed, norm):
        wide = src[...].astype(F32)
        n = jnp.sqrt(jnp.sum(wide * wide, axis=-1, keepdims=True) + 1e-06)
        out = wide / n
        normed[...] = out
        norm[...] = n
        return out.astype(BF)

    def part(ref, slot, count=1):
        return ref.at[pl.ds(pl.multiple_of(slot * HALF, HALF), HALF * count)]

    loads[0].wait()
    own_text = normalize(texts, tnormed, tnorm)
    part(tb, slot_at(0, 0, 0))[...] = own_text[0:HALF]
    part(tb, slot_at(0, 1, 0))[...] = own_text[HALF:]
    loads[1].wait()
    im[0, core] = normalize(images, inormed, inorm)

    pl.semaphore_wait(barrier, len(partners))

    pending = []
    numbers = iter(range(64))

    def put(src, dst, recv, device, cond=None):
        sem = send.at[next(numbers)]

        def make():
            return pltpu.make_async_remote_copy(
                src_ref=src(), dst_ref=dst(), send_sem=sem, recv_sem=recv(),
                device_id=device, device_id_type=MESH,
            )

        pending.append((make, cond))
        if cond is None:
            make().start()
        else:
            @pl.when(cond)
            def _():
                make().start()

    def drain(count):
        for make, cond in pending[:count]:
            if cond is None:
                make().wait_send()
            else:
                @pl.when(cond)
                def _():
                    make().wait_send()

        del pending[:count]

    def got(dst, recv, cond=None):
        def wait():
            pltpu.make_async_remote_copy(
                src_ref=dst(), dst_ref=dst(), send_sem=send.at[0], recv_sem=recv(),
                device_id=at(dc=1), device_id_type=MESH,
            ).wait_recv()

        if cond is None:
            wait()
        else:
            @pl.when(cond)
            def _():
                wait()

    def put_slot(src, dst, device, cond=None):
        put(lambda: part(tb, src), lambda: part(tb, dst), lambda: tb_r.at[dst], device, cond)

    def got_slot(slot, cond=None):
        got(lambda: part(tb, slot), lambda: tb_r.at[slot], cond)

    wraps = [(z + k >= 4).astype(jnp.int32) for k in range(4)]
    wrapped = [(z < k).astype(jnp.int32) for k in range(4)]

    own_low, own_high = slot_at(0, 0, 0), slot_at(0, 1, 0)

    def along_z_high(k):
        s = wraps[k]
        put_slot(own_high, s * (17 + k) + (1 - s) * slot_at(k, 1, 0), at(dz=k))

    def along_z_low(k):
        put_slot(own_low, slot_at(k, 0, 0), at(dz=k), wraps[k] == 0)

    def relay_z_near(d, order):
        got_slot(16 + d // 2, z > 0)
        for k in order:
            put_slot(16 + d // 2, slot_at(k, 0, d // 2), at(dz=k), wraps[k] == 1)

    def relay_z_far(order):
        got_slot(slot_at(0, 0, 1))
        for k in order:
            put_slot(slot_at(0, 0, 1), slot_at(k, 0, 1), at(dz=k), wraps[k] == 0)

    def relay_x(k):
        s = wrapped[k]
        here = s * (17 + k) + (1 - s) * slot_at(k, 1, 0)
        got_slot(here)
        put_slot(here, slot_at(k, 1, 1), at(dx=s + 2))
        put_slot(here, slot_at(k, 1, 0), at(dx=1), s == 1)

    def send_image(d, h):
        a = IMAGE_AT[d]
        rows = pl.ds(h * HALF, HALF)
        put(lambda: im.at[0, core, rows], lambda: im.at[a, core, rows], lambda: im_h.at[a, h], at(dy=d))

    def forward_image(d):
        a, b = IMAGE_AT[d], IMAGE_AT[2]
        h = d // 2
        rows = pl.ds(h * HALF, HALF)
        got(lambda: im.at[a, core, rows], lambda: im_h.at[a, h])
        put(lambda: im.at[a, core, rows], lambda: im.at[b, core, rows], lambda: im_h.at[b, h], at(dy=d))

    def relay_image(d):
        a = IMAGE_AT[d]
        for h in (0, 1):
            if d == 2 or d and h != d // 2:
                rows = pl.ds(h * HALF, HALF)
                got(lambda: im.at[a, core, rows], lambda: im_h.at[a, h])
        put(lambda: im.at[a, core], lambda: im.at[a, core], lambda: im_r.at[a], at(dc=1))

    def got_image(d):
        a = IMAGE_AT[d]
        got(lambda: im.at[a, 1 - core], lambda: im_r.at[a])

    scale = logit_scale[0]
    shift = bias[0]

    def early(k, first):
        base = CHUNK_AT[k] * 4 * HALF
        rows = pl.ds(base, 4 * HALF)
        t = tb[rows]
        i = im[0:3].reshape(EARLY, WIDTH)
        logits = scale * lax.dot_general(t, i, (((1,), (1,)), ((), ())), preferred_element_type=F32) + shift
        if k == 0:
            r = lax.broadcasted_iota(jnp.int32, logits.shape, 0)
            c = lax.broadcasted_iota(jnp.int32, logits.shape, 1)
            own = r // (2 * HALF) * HALF + r % HALF + core * ROWS
            positive = (c == own) & (r // HALF % 2 == 0)
            signs = jnp.where(positive, 1.0, -1.0).astype(F32)
            slopes = -signs / (1.0 + jnp.exp(signs * logits))
        else:
            slopes = 1.0 / (1.0 + jnp.exp(-logits))
        slopes = slopes.astype(BF)
        pt[rows] = jnp.dot(slopes, i, preferred_element_type=F32)
        term = lax.dot_general(slopes, t, (((0,), (0,)), ((), ())), preferred_element_type=F32)
        if first:
            di[0:EARLY] = term
        else:
            di[0:EARLY] += term

    def early_images(k):
        rows = pl.ds(CHUNK_AT[k] * 4 * HALF, 4 * HALF)
        t = tb[rows]
        i = im[0:3].reshape(EARLY, WIDTH)
        logits = scale * lax.dot_general(t, i, (((1,), (1,)), ((), ())), preferred_element_type=F32) + shift
        slopes = (1.0 / (1.0 + jnp.exp(-logits))).astype(BF)
        de[...] = slopes
        di[0:EARLY] += lax.dot_general(slopes, t, (((0,), (0,)), ((), ())), preferred_element_type=F32)

    def early_texts(k):
        rows = pl.ds(CHUNK_AT[k] * 4 * HALF, 4 * HALF)
        pt[rows] = jnp.dot(de[...], im[0:3].reshape(EARLY, WIDTH), preferred_element_type=F32)

    def late_images(ks):
        rows = pl.ds(CHUNK_AT[ks[0]] * 4 * HALF, 4 * HALF * len(ks))
        t = tb[rows]
        i = im[3].reshape(2 * ROWS, WIDTH)
        logits = scale * lax.dot_general(i, t, (((1,), (1,)), ((), ())), preferred_element_type=F32) + shift
        slopes = (1.0 / (1.0 + jnp.exp(-logits))).astype(BF)
        dl[...] = slopes
        di[EARLY:] += jnp.dot(slopes, t, preferred_element_type=F32)

    def late_texts(ks):
        rows = pl.ds(CHUNK_AT[ks[0]] * 4 * HALF, 4 * HALF * len(ks))
        i = im[3].reshape(2 * ROWS, WIDTH)
        term = lax.dot_general(dl[...], i, (((0,), (0,)), ((), ())), preferred_element_type=F32)
        pb[rows] = (pt[rows] + term).astype(BF)

    def late(ks, first):
        rows = pl.ds(CHUNK_AT[ks[0]] * 4 * HALF, 4 * HALF * len(ks))
        t = tb[rows]
        i = im[3].reshape(2 * ROWS, WIDTH)
        logits = scale * lax.dot_general(i, t, (((1,), (1,)), ((), ())), preferred_element_type=F32) + shift
        slopes = (1.0 / (1.0 + jnp.exp(-logits))).astype(BF)
        term = lax.dot_general(slopes, i, (((0,), (0,)), ((), ())), preferred_element_type=F32)
        pb[rows] = (pt[rows] + term).astype(BF)
        term = jnp.dot(slopes, t, preferred_element_type=F32)
        if first:
            di[EARLY:] = term
        else:
            di[EARLY:] += term

    def value(slot):
        return part(pb, slot)[...].astype(F32)

    def got_chunk(k):
        if k == 0:
            got_slot(slot_at(0, 1, 1))
            return
        got_slot(slot_at(k, 0, 0))
        got_slot(slot_at(k, 0, 1))
        got_slot(slot_at(k, 1, 0), wrapped[k] == 1)
        got_slot(slot_at(k, 1, 1))

    def send_chunk(k, order):
        if k == 0:
            put(lambda: part(pb, slot_at(0, 1, 1)), lambda: o1.at[0], lambda: o1_r.at[0], at(dx=2))
            return
        s = wrapped[k]
        for which in order:
            if which == "1":
                put(lambda: part(pb, slot_at(k, 1, 1)), lambda: zr.at[k - 1, 1], lambda: zr_r.at[k - 1, 1], at(dx=-s - 2))
            elif which == "0":
                put(lambda: part(pb, slot_at(k, 1, 0)), lambda: zr.at[k - 1, 0], lambda: zr_r.at[k - 1, 0], at(dx=-1), s == 1)
            else:
                put(lambda: part(pb, slot_at(k, 0, 0), 2), lambda: xr.at[k - 1], lambda: xr_r.at[k - 1], at(dz=-k))

    def collect_z(k):
        s = wrapped[k]
        got(lambda: zr.at[k - 1, 1], lambda: zr_r.at[k - 1, 1])
        got(lambda: zr.at[k - 1, 0], lambda: zr_r.at[k - 1, 0], s == 1)

        @pl.when(s == 1)
        def _():
            sf[...] = zr[k - 1, 1].astype(F32) + zr[k - 1, 0].astype(F32)

        @pl.when(s == 0)
        def _():
            sf[...] = zr[k - 1, 1].astype(F32) + value(slot_at(k, 1, 0))

        if k == 2:
            sz[k - 1] = sf[...].astype(BF)
            for h, d in ((0, 3), (1, 1)):
                rows = pl.ds(h * QUARTER, QUARTER)
                put(lambda rows=rows: sz.at[1, rows], lambda h=h: o2.at[h], lambda h=h: o2_r.at[h], at(dz=d))
            return
        h = k // 2
        rows = pl.ds(h * QUARTER, QUARTER)
        got(lambda: o2.at[h], lambda: o2_r.at[h])
        sf[rows] += o2[h].astype(F32)
        sz[k - 1] = sf[...].astype(BF)
        put(lambda: sz.at[k - 1], lambda: o1.at[k], lambda: o1_r.at[k], at(dz=-k))

    def di_rows(d, half):
        return pl.ds(pl.multiple_of(IMAGE_AT[d] * 2 * ROWS + half * ROWS, ROWS), ROWS)

    def swap_image(d):
        sd[d] = di[di_rows(d, 1 - core)].astype(BF)
        put(lambda: sd.at[d], lambda: dr.at[d], lambda: dr_r.at[d], at(dc=1))

    def mine(d):
        got(lambda: dr.at[d], lambda: dr_r.at[d])
        return di[di_rows(d, core)] + dr[d].astype(F32)

    def put_image(d, h):
        rows = pl.ds(h * HALF, HALF)
        put(lambda: sy.at[d - 1, rows], lambda: dyr.at[d // 2, rows], lambda: dy_r.at[d // 2, h], at(dy=-d))

    def return_images():
        sy[1] = mine(2).astype(BF)
        for h, d in ((0, 3), (1, 1)):
            rows = pl.ds(h * HALF, HALF)
            put(lambda rows=rows: sy.at[1, rows], lambda h=h: y2.at[h], lambda h=h: y2_r.at[h], at(dy=d))
        for d in (1, 3):
            sm[d // 2] = mine(d)
            h = 1 - d // 2
            sy[d - 1, pl.ds(h * HALF, HALF)] = sm[d // 2, pl.ds(h * HALF, HALF)].astype(BF)
            put_image(d, h)

    def return_sums():
        for d in (1, 3):
            h = d // 2
            rows = pl.ds(h * HALF, HALF)
            got(lambda: y2.at[h], lambda: y2_r.at[h])
            sy[d - 1, rows] = (sm[h, rows] + y2[h].astype(F32)).astype(BF)
            put_image(d, h)

    def column(j, wrap):
        total = None
        for k in (1, 2, 3):
            term = xr[k - 1, pl.ds(j * HALF, HALF)].astype(F32)
            term = jnp.where(wraps[k] == wrap, term, 0.0)
            total = term if total is None else total + term
        return total

    def got_column():
        for k in (1, 3, 2):
            got(lambda k=k: xr.at[k - 1], lambda k=k: xr_r.at[k - 1])

    def collect_far():
        sx[1] = (column(1, 0) + value(slot_at(0, 0, 1))).astype(BF)
        put(lambda: sx.at[1], lambda: o0.at[1], lambda: o0_r.at[1], at(dx=-2))

    def collect_near():
        for d in (1, 3):
            @pl.when(z > 0)
            def _():
                sx[d - 1] = column(d // 2, 1).astype(BF)

            put(lambda d=d: sx.at[d - 1], lambda d=d: o0.at[d - 1], lambda d=d: o0_r.at[d - 1], at(dx=-d), z > 0)

    def unnormalize(normed, norm, upstream):
        inner = jnp.sum(normed * upstream, axis=-1, keepdims=True)
        return (upstream - normed * inner) / norm

    along_z_high(2)
    along_z_high(1)
    along_z_high(3)
    for d, h in ((1, 0), (3, 1), (1, 1), (3, 0)):
        send_image(d, h)
    put_slot(own_low, 16, at(dx=1), z > 0)
    put_slot(own_low, 17, at(dx=3), z > 0)
    put_slot(own_low, slot_at(0, 0, 1), at(dx=2))
    along_z_low(2)
    put_slot(own_high, slot_at(0, 1, 1), at(dx=2))
    along_z_low(3)
    relay_image(0)
    relay_x(3)
    relay_z_near(1, (3, 1, 2))
    relay_z_near(3, (3, 1, 2))
    relay_z_far((2, 1, 3))
    along_z_low(1)
    forward_image(1)
    forward_image(3)
    relay_image(1)
    relay_image(3)
    relay_x(2)
    relay_image(2)
    relay_x(1)
    got_chunk(0)
    for d in (0, 1, 3):
        got_image(d)
    early(0, True)
    got_chunk(3)
    early(3, False)
    got_chunk(2)
    early(2, False)
    got_image(2)
    late((2,), True)
    send_chunk(2, "10x")
    late((3,), False)
    send_chunk(3, "10x")
    got_chunk(1)
    late_images((0, 1))
    swap_image(2)
    early_images(1)
    for d in (1, 3, 0):
        swap_image(d)
    early_texts(1)
    late_texts((0, 1))
    send_chunk(0, "10x")
    send_chunk(1, "10x")
    return_images()
    collect_z(2)
    return_sums()
    got_column()
    collect_far()
    collect_near()
    collect_z(1)
    collect_z(3)

    total = mine(0)
    for d in (1, 3):
        for h in (0, 1):
            rows = pl.ds(h * HALF, HALF)
            got(lambda: dyr.at[d // 2, rows], lambda: dy_r.at[d // 2, h])
        total = total + dyr[d // 2].astype(F32)
    grad_images[...] = unnormalize(inormed[...], inorm[...], total)

    lower = column(0, 0) + value(slot_at(0, 0, 0))
    got(lambda: o0.at[1], lambda: o0_r.at[1])
    lower = lower + o0[1].astype(F32)
    for d in (1, 3):
        got(lambda d=d: o0.at[d - 1], lambda d=d: o0_r.at[d - 1], z > 0)
        lower = lower + jnp.where(z > 0, o0[d - 1].astype(F32), 0.0)
    upper = value(slot_at(0, 1, 0))
    for k in (0, 1, 3):
        got(lambda k=k: o1.at[k], lambda k=k: o1_r.at[k])
        upper = upper + o1[k].astype(F32)
    grad_texts[0:HALF] = unnormalize(tnormed[0:HALF], tnorm[0:HALF], lower)
    grad_texts[HALF:] = unnormalize(tnormed[HALF:], tnorm[HALF:], upper)

    drain(len(pending))


def local(images, texts, logit_scale, bias):
    hbm = pl.BlockSpec(memory_space=pl.ANY)
    vmem = pl.BlockSpec(memory_space=pltpu.VMEM)
    smem = pl.BlockSpec(memory_space=pltpu.SMEM)
    dma = pltpu.SemaphoreType.DMA
    grads = pl.pallas_call(
        kernel,
        out_shape=[pltpu.VMEM((ROWS, WIDTH), F32)] * 2,
        in_specs=[smem, smem, hbm, hbm],
        out_specs=[vmem, vmem],
        scratch_shapes=[
            pltpu.VMEM((ROWS, WIDTH), BF),
            pltpu.VMEM((ROWS, WIDTH), BF),
            pltpu.VMEM((ROWS, WIDTH), F32),
            pltpu.VMEM((ROWS, WIDTH), F32),
            pltpu.VMEM((ROWS, 1), F32),
            pltpu.VMEM((ROWS, 1), F32),
            pltpu.VMEM((4, 2, ROWS, WIDTH), BF),
            pltpu.VMEM((21 * HALF, WIDTH), BF),
            pltpu.VMEM((8 * ROWS, WIDTH), F32),
            pltpu.VMEM((16 * HALF, WIDTH), F32),
            pltpu.VMEM((16 * HALF, WIDTH), BF),
            pltpu.VMEM((3, 2 * HALF, WIDTH), BF),
            pltpu.VMEM((3, 2, HALF, WIDTH), BF),
            pltpu.VMEM((3, HALF, WIDTH), BF),
            pltpu.VMEM((4, HALF, WIDTH), BF),
            pltpu.VMEM((4, ROWS, WIDTH), BF),
            pltpu.VMEM((3, ROWS, WIDTH), BF),
            pltpu.VMEM((3, HALF, WIDTH), BF),
            pltpu.VMEM((3, HALF, WIDTH), BF),
            pltpu.VMEM((4, ROWS, WIDTH), BF),
            pltpu.VMEM((3, ROWS, WIDTH), BF),
            pltpu.VMEM((HALF, WIDTH), F32),
            pltpu.VMEM((2, QUARTER, WIDTH), BF),
            pltpu.VMEM((4 * HALF, EARLY), BF),
            pltpu.VMEM((2 * ROWS, 8 * HALF), BF),
            pltpu.VMEM((2, HALF, WIDTH), BF),
            pltpu.VMEM((2, ROWS, WIDTH), F32),
            dma((2,)),
            dma((2,)),
            dma((2,)),
            dma((64,)),
            dma((4, 2)),
            dma((4,)),
            dma((21,)),
            dma((3,)),
            dma((3, 2)),
            dma((3,)),
            dma((4,)),
            dma((4,)),
            dma((2, 2)),
        ],
        compiler_params=pltpu.CompilerParams(
            collective_id=0, has_side_effects=True, vmem_limit_bytes=56 * 2**20
        ),
        name="pair_grads",
    )(logit_scale, bias, images, texts)
    return tuple(logit_scale[0] * grad for grad in grads)


def solution(mesh):
    in_specs = (P(("loop", "group"), None), P(("loop", "group"), None), P(), P())
    out_specs = (P(("loop", "group"), None), P(("loop", "group"), None))
    return jax.shard_map(local, mesh=mesh, in_specs=in_specs, out_specs=out_specs, check_vma=False)
```
